128 devices in a mesh: ctx: 64 (over x, z_hi, y, core), ch: 2 (over z_lo).
Axes of the slice: x: 4, y: 4, z: 4 (z_hi: 2, z_lo: 2; z = z_hi * 2 + z_lo), core: 2. Of those that a mesh axis runs over, the one named last changes fastest.
Arguments:
- tokens: bfloat16 [512, 512, 1536], P('ctx', None, 'ch'), may hold values from -6 to 6
- mix_first: bfloat16 [512, 512], replicated, may hold values from -0.25 to 0.25
- mix_second: bfloat16 [512, 512], replicated, may hold values from -0.25 to 0.25
- spectral_kernel: bfloat16 [512, 512, 1536], P('ctx', None, 'ch'), may hold values from -6 to 6
- gate_scale: float32 [1536], P('ch'), may hold values from 0.25 to 4
- up_weight: bfloat16 [4, 384, 4, 384], P('ch'), may hold values from -0.3125 to 0.3125
- down_weight: bfloat16 [4, 384, 4, 384], P('ch'), may hold values from -0.15625 to 0.15625
- first_exponents: int32 [512, 512, 12], P('ctx', None, 'ch'), may hold values from -9 to 2
- second_exponents: int32 [512, 512, 12], P(None, 'ctx', 'ch'), may hold values from -9 to 2
Outputs:
- layer_out: bfloat16 [512, 512, 1536], P('ctx', None, 'ch')
The draws below stay inside these ranges and needn't reach their ends.
Inputs may be any that keep to these rules, and one draw needn't show every extreme that they name: `first_exponents`: power-of-two exponent of a block of 128 channels at one position. `second_exponents`: power-of-two exponent of a block of 128 channels at one position.
All inputs are finite; a program needn't handle non-finite values.
Results may differ from the reference program's by a relative error of at most 0.01.
Values may be sent and summed in bfloat16 or wider, within the bound.
No kernel may reach another device: no remote copies, remote signals or barrier semaphores. Data moves between devices by JAX's collectives and lax.ppermute only.
A program may use at most 192 MiB of HBM per device.

```python
import math
import jax
import jax.numpy as jnp
from jax import lax

P_SIZE = 512
Q = 512
D = 1536
BLK = 128
NBLK = 4
BW = 384
N_CH = 2


def plant(drawn, rng, low, top_value):
    extent = drawn.shape
    index_at = [jax.random.randint(jax.random.fold_in(rng, axis), (), 0, extent[axis]) for axis in range(len(extent))]
    drawn = drawn.at[tuple(index_at)].set(low)
    longest = extent.index(max(extent))
    index_at[longest] = (index_at[longest] + 1) % extent[longest]
    return drawn.at[tuple(index_at)].set(top_value)


def block_levels(key, dims, split, low, largest):
    factor_of = 1.0
    for position, blocks in split:
        heights = jax.random.uniform(jax.random.fold_in(jax.random.fold_in(key, 6), position), (blocks,), jnp.float32, low / len(split), largest / len(split))
        factor_of = factor_of * jnp.repeat(jnp.exp(heights), dims[position] // blocks).reshape((-1,) + (1,) * (len(dims) - 1 - position))
    return factor_of


def noise(stream_key, dims, deviation, most, cuts=(), dtype=jnp.bfloat16):
    level = block_levels(stream_key, dims, cuts, -0.22, 0.18) if cuts else 1.0
    array = jax.random.normal(stream_key, dims, jnp.float32) * deviation * level
    return jnp.minimum(jnp.maximum(array, -most), most).astype(dtype)


def setup_inputs(seed: int = 0) -> dict:
    seeds = jax.random.split(jax.random.key(seed), 10)
    tokens = noise(seeds[0], (P_SIZE, Q, D), 1.0, 6.0, ((0, 64), (2, 2)))
    mix_first = noise(seeds[1], (Q, Q), Q ** -0.5, 0.25)
    mix_second = noise(seeds[2], (P_SIZE, P_SIZE), P_SIZE ** -0.5, 0.25)
    spectral_kernel = noise(seeds[3], (P_SIZE, Q, D), 1.0, 6.0, ((0, 64), (2, 2)))
    gate_scale = jnp.clip(jnp.exp(math.log(4.0) - 2.7725887 * jax.random.uniform(seeds[4], (D,), jnp.float32) ** block_levels(seeds[4], (D,), ((0, 2),), -0.2, 0.2)), 0.25, 4.0)
    up_weight = noise(seeds[5], (NBLK, BW, NBLK, BW), BW ** -0.5, 0.3125, ((0, 2),))
    down_weight = noise(seeds[6], (NBLK, BW, NBLK, BW), (NBLK * BW) ** -0.5, 0.15625, ((0, 2),))
    first_exponents = plant(jax.random.randint(seeds[7], (P_SIZE, Q, D // BLK), -9, 3), jax.random.fold_in(seeds[7], 1), -9, 2).astype(jnp.int32)
    second_exponents = plant(jax.random.randint(seeds[8], (P_SIZE, Q, D // BLK), -9, 3), jax.random.fold_in(seeds[8], 1), -9, 2).astype(jnp.int32)
    return {"tokens": tokens, "mix_first": mix_first, "mix_second": mix_second, "spectral_kernel": spectral_kernel, "gate_scale": gate_scale, "up_weight": up_weight, "down_weight": down_weight, "first_exponents": first_exponents, "second_exponents": second_exponents}


exp_low = -9
exp_high = 3
clip_top = 448.0


def power_table(exponent, sign_of):
    result = jnp.zeros(exponent.shape, jnp.float32)
    for power_k in range(exp_low, exp_high):
        result = result + jnp.where(exponent == power_k, 2.0 ** (sign_of * power_k), 0.0).astype(jnp.float32)
    return result


def round_trip(values, exponent):
    shaped = values.reshape(values.shape[:-1] + (values.shape[-1] // BLK, BLK))
    encoded = jnp.clip(shaped * power_table(exponent, -1)[..., None], -clip_top, clip_top).astype(jnp.bfloat16)
    encoded = lax.optimization_barrier(encoded)
    decoded = (encoded.astype(jnp.float32) * power_table(exponent, 1)[..., None]).astype(jnp.bfloat16)
    return decoded.reshape(values.shape)


def reference(tokens, mix_first, mix_second, spectral_kernel, gate_scale, up_weight, down_weight, first_exponents, second_exponents):
    step_rows = 8
    left_mix = mix_first.astype(jnp.float32)
    right_mix = mix_second.astype(jnp.float32)
    up_float = up_weight.astype(jnp.float32)
    down_float = down_weight.astype(jnp.float32)

    def first_block(pieces):
        tok_block, kernel_block, exp_block = pieces
        first_mix = jnp.einsum('qr,prd->pqd', left_mix, tok_block.astype(jnp.float32))
        return round_trip(first_mix * kernel_block.astype(jnp.float32), exp_block)

    got_first = lax.map(first_block, (tokens.reshape(P_SIZE // step_rows, step_rows, Q, D),
                                      spectral_kernel.reshape(P_SIZE // step_rows, step_rows, Q, D),
                                      first_exponents.reshape(P_SIZE // step_rows, step_rows, Q, D // BLK)))
    got_first = got_first.reshape(P_SIZE, Q, D)
    columns = got_first.reshape(P_SIZE, Q // step_rows, step_rows, D).transpose(1, 0, 2, 3)
    column_exps = second_exponents.reshape(P_SIZE, Q // step_rows, step_rows, D // BLK).transpose(1, 0, 2, 3)

    def second_block(pieces):
        col_block, exp_block = pieces
        second_mix = jnp.einsum('pr,rqd->pqd', right_mix, col_block.astype(jnp.float32))
        return round_trip(second_mix, exp_block)

    mixed_seq = lax.map(second_block, (columns, column_exps)).transpose(1, 0, 2, 3).reshape(P_SIZE, Q, D)

    def third_block(pieces):
        tok_block, mixed_block = pieces
        plain_tok = tok_block.astype(jnp.float32)
        gated_seq = (plain_tok + mixed_block.astype(jnp.float32) * jax.nn.sigmoid(plain_tok * gate_scale)).astype(jnp.bfloat16)
        token_rows = gated_seq.reshape(-1, NBLK, BW).astype(jnp.float32)
        hidden = jax.nn.gelu(jnp.einsum('tic,icks->tiks', token_rows, up_float), approximate=True).astype(jnp.bfloat16)
        hidden = lax.optimization_barrier(hidden).astype(jnp.float32)
        running = jnp.zeros((token_rows.shape[0], NBLK, BW), jnp.float32)
        group_size = NBLK // N_CH
        for group_idx in range(N_CH):
            low = group_idx * group_size
            partial_value = jnp.einsum('tiks,isko->tko', hidden[:, low:low + group_size], down_float[low:low + group_size])
            running = running + lax.optimization_barrier(partial_value.astype(jnp.bfloat16)).astype(jnp.float32)
        return (token_rows + running).reshape(tok_block.shape).astype(jnp.bfloat16)

    layer_out = lax.map(third_block, (tokens.reshape(P_SIZE // step_rows, step_rows, Q, D),
                                      mixed_seq.reshape(P_SIZE // step_rows, step_rows, Q, D)))
    return layer_out.reshape(P_SIZE, Q, D)
```

```python
import functools

import jax
import jax.numpy as jnp
import numpy as np
from jax import lax
from jax.experimental import pallas as pl
from jax.experimental.pallas import tpu as pltpu
from jax.sharding import PartitionSpec as P

BLK = 128
HALF = 768
BW = 384
WIDE = 1536
VMEM = 56 * 1024 * 1024
BOTH = ("ctx", "ch")


def limits(exponent):
    return lax.shift_left(jnp.ones_like(exponent), exponent + 9).astype(jnp.float32) * 0.875


def regroup_matrix():
    matrix = np.zeros((256, 256), np.float32)
    for r in range(4):
        for j in range(8):
            for a in range(8):
                matrix[r * 64 + j * 8 + a, a * 32 + j * 4 + r] = 1.0
    return matrix


def first_kernel(mix_ref, perm_ref, tok_ref, spec_ref, exp_ref, out0_ref, out1_ref, enc_ref):
    columns = limits(exp_ref[0]).T
    mix = mix_ref[...]
    for pair in range(4):
        rhs = jnp.concatenate([tok_ref[2 * pair], tok_ref[2 * pair + 1]], axis=1)
        acc = jnp.dot(mix, rhs, preferred_element_type=jnp.float32)
        for side in range(2):
            a = 2 * pair + side
            value = acc[:, side * BLK:(side + 1) * BLK] * spec_ref[a].astype(jnp.float32)
            top = columns[:, a:a + 1]
            enc_ref[a] = jnp.clip(value, -top, top).astype(jnp.bfloat16)

    def regroup(g, carry):
        rows = pl.ds(pl.multiple_of(g * 32, 32), 32)
        both = jnp.concatenate(
            [enc_ref[:, rows, :].reshape(256, BLK), tok_ref[:, rows, :].reshape(256, BLK)], axis=1
        )
        moved = jnp.dot(perm_ref[...], both, preferred_element_type=jnp.float32)
        dest = pl.ds(pl.multiple_of(g * 8, 8), 8)
        for r in range(4):
            out_ref = (out0_ref, out1_ref)[r // 2]
            part = moved[r * 64:(r + 1) * 64]
            for t in range(2):
                out_ref[dest, r % 2, t] = (
                    part[:, t * BLK:(t + 1) * BLK].reshape(8, 8, BLK).astype(jnp.bfloat16)
                )
        return carry

    lax.fori_loop(0, 16, regroup, 0, unroll=4)


def first_stage(mix_first, perm, tokens, spectral, exponents):
    out = jax.ShapeDtypeStruct((128, 2, 2, 8, HALF), jnp.bfloat16)
    out_spec = pl.BlockSpec((128, 2, 2, 8, BLK), lambda d: (0, 0, 0, 0, d))
    wide = pl.BlockSpec((8, 512, BLK), lambda d: (0, 0, d))
    return pl.pallas_call(
        first_kernel,
        grid=(HALF // BLK,),
        in_specs=[
            pl.BlockSpec((512, 512), lambda d: (0, 0)),
            pl.BlockSpec((256, 256), lambda d: (0, 0)),
            wide,
            wide,
            pl.BlockSpec((1, 8, 512), lambda d: (d, 0, 0)),
        ],
        out_specs=[out_spec, out_spec],
        out_shape=[out, out],
        scratch_shapes=[pltpu.VMEM((8, 512, BLK), jnp.bfloat16)],
        compiler_params=pltpu.CompilerParams(vmem_limit_bytes=VMEM),
        cost_estimate=pl.CostEstimate(flops=6_400_000_000, bytes_accessed=25_200_000, transcendentals=0),
        name="first_mix",
    )(mix_first, perm, tokens, spectral, exponents)


def mixer_kernel(mix_ref, recv_ref, top_ref, gate_ref, up_ref, down_ref, out_ref, gated_ref):
    m = pl.program_id(1)
    lead = pl.ds(pl.multiple_of(m * 32, 32), 32)
    for c in range(2):
        right = recv_ref[:, c, 0, 0].reshape(512, HALF)
        mixed = jnp.dot(mix_ref[...], right, preferred_element_type=jnp.float32)
        tok = recv_ref[lead, c, 0, 1].reshape(256, HALF).astype(jnp.float32)
        slope = jax.nn.sigmoid(tok * gate_ref[c:c + 1, :])
        for n in range(6):
            cols = slice(n * BLK, (n + 1) * BLK)
            top = top_ref[0, :, c * 6 + n:c * 6 + n + 1]
            held = jnp.clip(mixed[:, cols], -top, top).astype(jnp.bfloat16).astype(jnp.float32)
            gated_ref[:, c * HALF + n * BLK:c * HALF + (n + 1) * BLK] = (
                tok[:, cols] + held * slope[:, cols]
            ).astype(jnp.bfloat16)
    totals = [None] * 4
    for i in range(4):
        pre = jnp.dot(
            gated_ref[:, i * BW:(i + 1) * BW], up_ref[i], preferred_element_type=jnp.float32
        )
        hidden = jax.nn.gelu(pre, approximate=True).astype(jnp.bfloat16)
        for k in range(4):
            cols = slice(k * BW, (k + 1) * BW)
            part = jnp.dot(hidden[:, cols], down_ref[i, :, cols], preferred_element_type=jnp.float32)
            totals[k] = part if i == 0 else totals[k] + part
    for k in range(4):
        result = (gated_ref[:, k * BW:(k + 1) * BW].astype(jnp.float32) + totals[k]).astype(jnp.bfloat16)
        out_ref[:, k // 2, 0, :, (k % 2) * BW:(k % 2 + 1) * BW] = result.reshape(32, 8, BW)


def mixer_stage(mix_second, received, tops, gate, up, down):
    fixed = pl.BlockSpec((4, BW, WIDE), lambda q, m: (0, 0, 0))
    return pl.pallas_call(
        mixer_kernel,
        grid=(2, 2),
        in_specs=[
            pl.BlockSpec((256, 512), lambda q, m: (m, 0)),
            pl.BlockSpec((64, 2, 1, 2, 8, HALF), lambda q, m: (0, 0, q, 0, 0, 0)),
            pl.BlockSpec((1, 256, 12), lambda q, m: (q, m, 0)),
            pl.BlockSpec((2, HALF), lambda q, m: (0, 0)),
            fixed,
            fixed,
        ],
        out_specs=pl.BlockSpec((32, 2, 1, 8, HALF), lambda q, m: (m, 0, q, 0, 0)),
        out_shape=jax.ShapeDtypeStruct((64, 2, 2, 8, HALF), jnp.bfloat16),
        scratch_shapes=[pltpu.VMEM((256, WIDE), jnp.bfloat16)],
        compiler_params=pltpu.CompilerParams(vmem_limit_bytes=VMEM),
        cost_estimate=pl.CostEstimate(
            flops=12_000_000_000, bytes_accessed=19_000_000, transcendentals=8_000_000
        ),
        name="second_mix_and_channel_mix",
    )(mix_second, received, tops, gate, up, down)


def last_kernel(perm_ref, in0_ref, in1_ref, out_ref):
    def regroup(g, carry):
        parts = []
        for u in range(2):
            source = pl.ds(pl.multiple_of(g * 16 + u * 8, 8), 8)
            rows = [(in0_ref, in1_ref)[r // 2][source, r % 2].reshape(64, BLK) for r in range(4)]
            parts.append(jnp.concatenate(rows, axis=0))
        moved = jnp.dot(perm_ref[...], jnp.concatenate(parts, axis=1), preferred_element_type=jnp.float32)
        for u in range(2):
            dest = pl.ds(pl.multiple_of(g * 64 + u * 32, 32), 32)
            out_ref[:, dest, :] = (
                moved[:, u * BLK:(u + 1) * BLK].reshape(8, 32, BLK).astype(jnp.bfloat16)
            )
        return carry

    lax.fori_loop(0, 8, regroup, 0, unroll=4)


def last_stage(perm, part0, part1):
    block = pl.BlockSpec((128, 2, 8, BLK), lambda d: (0, 0, 0, d))
    return pl.pallas_call(
        last_kernel,
        grid=(HALF // BLK,),
        in_specs=[pl.BlockSpec((256, 256), lambda d: (0, 0)), block, block],
        out_specs=pl.BlockSpec((8, 512, BLK), lambda d: (0, 0, d)),
        out_shape=jax.ShapeDtypeStruct((8, 512, HALF), jnp.bfloat16),
        compiler_params=pltpu.CompilerParams(vmem_limit_bytes=VMEM),
        cost_estimate=pl.CostEstimate(flops=1_600_000_000, bytes_accessed=12_600_000, transcendentals=0),
        name="regroup_result",
    )(perm, part0, part1)


def swap(value):
    return lax.ppermute(value, "ch", [(0, 1), (1, 0)])


def whole_weight(weight, ch):
    rows = weight.shape[0] * weight.shape[1]
    size = lax.axis_size("ctx")
    flat = weight.reshape(rows, weight.shape[2] * weight.shape[3])
    piece = rows // size
    start = lax.axis_index("ctx") * piece
    mine = lax.dynamic_slice_in_dim(weight.reshape(rows, 4, BW), start, piece, 0).reshape(piece, -1)
    other = lax.all_gather(swap(mine), "ctx", axis=0, tiled=True)
    low = jnp.where(ch == 0, flat, other)
    high = jnp.where(ch == 0, other, flat)
    return jnp.concatenate([low, high], axis=0).reshape(4, BW, WIDE)


def body(
    tokens,
    mix_first,
    mix_second,
    spectral_kernel,
    gate_scale,
    up_weight,
    down_weight,
    first_exponents,
    second_exponents,
):
    ch = lax.axis_index("ch")
    perm = regroup_matrix()
    send0, send1 = first_stage(
        mix_first,
        jnp.asarray(perm, jnp.bfloat16),
        tokens,
        spectral_kernel,
        first_exponents.transpose(2, 0, 1),
    )
    exchange = functools.partial(
        lax.all_to_all, axis_name=BOTH, split_axis=0, concat_axis=0, tiled=True
    )
    up = whole_weight(up_weight, ch)
    down = whole_weight(down_weight, ch)
    own_gate = gate_scale.reshape(1, HALF)
    other_gate = swap(own_gate)
    gate = jnp.where(
        ch == 0,
        jnp.concatenate([own_gate, other_gate], axis=0),
        jnp.concatenate([other_gate, own_gate], axis=0),
    )
    columns = second_exponents.transpose(2, 1, 0)
    mine = lax.dynamic_slice_in_dim(columns, 4 * ch, 4, 1)
    other = swap(lax.dynamic_slice_in_dim(columns, 4 * (1 - ch), 4, 1))
    exps = jnp.where(
        ch == 0, jnp.concatenate([mine, other], axis=0), jnp.concatenate([other, mine], axis=0)
    )
    tops = limits(exps.transpose(1, 2, 0))
    back = []
    for h, send in enumerate((send0, send1)):
        received = exchange(send).reshape(64, 2, 2, 2, 8, HALF)
        mixed = mixer_stage(mix_second, received, tops[2 * h:2 * h + 2], gate, up, down)
        back.append(exchange(mixed.reshape(128, 2, 8, HALF)))
    return last_stage(jnp.asarray(perm.T, jnp.bfloat16), back[0], back[1])


def solution(mesh):
    placed = (
        P("ctx", None, "ch"),
        P(),
        P(),
        P("ctx", None, "ch"),
        P("ch"),
        P("ch", None, None, None),
        P("ch", None, None, None),
        P("ctx", None, "ch"),
        P(None, "ctx", "ch"),
    )
    return jax.shard_map(
        body, mesh=mesh, in_specs=placed, out_specs=P("ctx", None, "ch"), check_vma=False
    )
```

```python
import jax
import jax.numpy as jnp
import numpy as np
from jax import lax
from jax.experimental import pallas as pl
from jax.experimental.pallas import tpu as pltpu
from jax.sharding import PartitionSpec as P


BLK = 128
HALF = 768
BW = 384
WIDE = 1536
VMEM = 56 * 1024 * 1024
BOTH = ("ctx", "ch")
N_CTX = 64


def z_hi(i):
    return (i // 8) % 2


SIDES = [[2 * i + (s ^ z_hi(i)) for i in range(N_CTX)] for s in range(2)]
PLANES = [[i for i in range(N_CTX) if z_hi(i) == z and i % 2 == core] for z in range(2) for core in range(2)]


def limits(exponent):
    return lax.shift_left(jnp.ones_like(exponent), exponent + 9).astype(jnp.float32) * 0.875


def regroup_matrix():
    matrix = np.zeros((256, 256), np.float32)
    for i in range(16):
        for r in range(2):
            for a in range(8):
                matrix[i * 16 + r * 8 + a, a * 32 + i * 2 + r] = 1.0
    return matrix


def first_kernel(mix_ref, perm_ref, tok_ref, spec_ref, exp_ref, out_ref, enc_ref):
    columns = limits(exp_ref[0]).T
    mix = mix_ref[...]
    for pair in range(4):
        rhs = jnp.concatenate([tok_ref[2 * pair], tok_ref[2 * pair + 1]], axis=1)
        acc = jnp.dot(mix, rhs, preferred_element_type=jnp.float32)
        for side in range(2):
            a = 2 * pair + side
            value = acc[:, side * BLK:(side + 1) * BLK] * spec_ref[a].astype(jnp.float32)
            top = columns[:, a:a + 1]
            enc_ref[a] = jnp.clip(value, -top, top).astype(jnp.bfloat16)
    for g in range(4):
        for h in range(2):
            both = jnp.concatenate(
                [
                    enc_ref[:, s * 256 + h * 128 + g * 32:s * 256 + h * 128 + (g + 1) * 32, :].reshape(256, BLK)
                    for s in range(2)
                ],
                axis=1,
            )
            moved = jnp.dot(perm_ref[...], both, preferred_element_type=jnp.float32).astype(jnp.bfloat16)
            for s in range(2):
                cols = slice(s * BLK, (s + 1) * BLK)
                out_ref[g * 16:g * 16 + 8, s, h] = moved[:128, cols].reshape(8, 16, BLK)
                out_ref[g * 16 + 8:g * 16 + 16, 1 - s, h] = moved[128:, cols].reshape(8, 16, BLK)


def first_stage(mix_first, perm, tokens, spectral, exponents):
    wide = pl.BlockSpec((8, 512, BLK), lambda d: (0, 0, d))
    return pl.pallas_call(
        first_kernel,
        grid=(HALF // BLK,),
        in_specs=[
            pl.BlockSpec((512, 512), lambda d: (0, 0)),
            pl.BlockSpec((256, 256), lambda d: (0, 0)),
            wide,
            wide,
            pl.BlockSpec((1, 8, 512), lambda d: (d, 0, 0)),
        ],
        out_specs=pl.BlockSpec((N_CTX, 2, 2, 16, BLK), lambda d: (0, 0, 0, 0, d)),
        out_shape=jax.ShapeDtypeStruct((N_CTX, 2, 2, 16, HALF), jnp.bfloat16),
        scratch_shapes=[pltpu.VMEM((8, 512, BLK), jnp.bfloat16)],
        compiler_params=pltpu.CompilerParams(vmem_limit_bytes=VMEM),
        cost_estimate=pl.CostEstimate(flops=4_800_000_000, bytes_accessed=18_900_000, transcendentals=0),
        name="first_mix",
    )(mix_first, perm, tokens, spectral, exponents)


def second_kernel(mix_ref, recv_ref, exp_ref, out_ref):
    columns = limits(exp_ref[0, 0]).T
    right = recv_ref[:, 0, 0].reshape(1024, 256)
    for m in range(4):
        rows = slice(m * 256, (m + 1) * 256)
        acc = jnp.dot(mix_ref[rows, :], right, preferred_element_type=jnp.float32)
        for n in range(2):
            top = columns[rows, n:n + 1]
            held = jnp.clip(acc[:, n * BLK:(n + 1) * BLK], -top, top).astype(jnp.bfloat16)
            out_ref[m * 16:(m + 1) * 16, :, n * BLK:(n + 1) * BLK] = held.reshape(16, 16, BLK)


def second_stage(mix, received, exponents, h):
    return pl.pallas_call(
        second_kernel,
        grid=(6,),
        in_specs=[
            pl.BlockSpec((1024, 1024), lambda n: (0, 0)),
            pl.BlockSpec((N_CTX, 1, 1, 16, 256), lambda n: (0, n // 3, h, 0, n % 3)),
            pl.BlockSpec((1, 1, 2, 1024), lambda n: (h, n, 0, 0)),
        ],
        out_specs=pl.BlockSpec((N_CTX, 16, 256), lambda n: (0, 0, n)),
        out_shape=jax.ShapeDtypeStruct((N_CTX, 16, WIDE), jnp.bfloat16),
        compiler_params=pltpu.CompilerParams(vmem_limit_bytes=VMEM),
        cost_estimate=pl.CostEstimate(flops=3_200_000_000, bytes_accessed=8_400_000, transcendentals=0),
        name="second_mix",
    )(mix, received, exponents)


def peel_kernel(place_ref, tok_ref, after_ref, out0_ref, out1_ref):
    del place_ref, after_ref
    out0_ref[...] = tok_ref[:, :128, :]
    out1_ref[...] = tok_ref[:, 128:, :]


def peel_stage(place, tokens, after):
    out = jax.ShapeDtypeStruct((8, 128, HALF), jnp.bfloat16)
    out_spec = pl.BlockSpec((8, 128, 256), lambda d, place: (0, 0, d))
    return pl.pallas_call(
        peel_kernel,
        grid_spec=pltpu.PrefetchScalarGridSpec(
            num_scalar_prefetch=1,
            grid=(3,),
            in_specs=[
                pl.BlockSpec((8, 256, 256), lambda d, place: (0, 1 - place[0], d)),
                pl.BlockSpec(memory_space=pl.ANY),
            ],
            out_specs=[out_spec, out_spec],
        ),
        out_shape=[out, out],
        compiler_params=pltpu.CompilerParams(vmem_limit_bytes=VMEM),
        cost_estimate=pl.CostEstimate(flops=0, bytes_accessed=6_300_000, transcendentals=0),
        name="tokens_to_send",
    )(place, tokens, after)


def mixer_kernel(
    place_ref, perm_ref, recv_ref, own_tok_ref, far_tok_ref, own_gate_ref, far_gate_ref,
    own_up_ref, far_up_ref, own_down_ref, far_down_ref, *rest
):
    own_out_ref, far_out_ref, gated_ref = rest[-3:]
    c = place_ref[1]
    toks = (own_tok_ref, far_tok_ref)
    gates = (own_gate_ref, far_gate_ref)
    ups = (own_up_ref, far_up_ref)
    downs = (own_down_ref, far_down_ref)
    starts = (pl.multiple_of(c * HALF, BLK), pl.multiple_of((1 - c) * HALF, BLK))
    for p in range(2):
        mixed = jnp.dot(
            perm_ref[...],
            recv_ref[:, :, pl.ds(starts[p], HALF)].reshape(256, HALF),
            preferred_element_type=jnp.float32,
        )
        tok = toks[p][...].reshape(256, HALF).astype(jnp.float32)
        slope = jax.nn.sigmoid(tok * gates[p][...])
        gated_ref[p] = (tok + mixed * slope).astype(jnp.bfloat16)
    for q in range(2):
        totals = [None, None]
        for p in range(2):
            hidden = []
            for i in range(2):
                pre = jnp.dot(
                    gated_ref[p, :, i * BW:(i + 1) * BW],
                    ups[p][i, :, pl.ds(starts[q], HALF)],
                    preferred_element_type=jnp.float32,
                )
                hidden.append(jax.nn.gelu(pre, approximate=True).astype(jnp.bfloat16))
            for k in range(2):
                left = jnp.concatenate([part[:, k * BW:(k + 1) * BW] for part in hidden], axis=1)
                right = downs[p][:, :, pl.ds(pl.multiple_of(starts[q] + k * BW, BLK), BW)].reshape(HALF, BW)
                part = jnp.dot(left, right, preferred_element_type=jnp.float32)
                totals[k] = part if p == 0 else totals[k] + part
        out_ref = (own_out_ref, far_out_ref)[q]
        for k in range(2):
            cols = slice(k * BW, (k + 1) * BW)
            result = gated_ref[q, :, cols].astype(jnp.float32) + totals[k]
            out_ref[:, :, cols] = result.astype(jnp.bfloat16).reshape(8, 32, BW)


def mixer_stage(place, perm, received, tokens, far_tokens, gates, ups, downs, whole, h, u):
    weight = pl.BlockSpec((2, BW, WIDE), lambda p, place: (0, 0, 0))
    gate = pl.BlockSpec((1, HALF), lambda p, place: (0, 0))
    own = pl.BlockSpec((8, 32, HALF), lambda p, place: (0, 8 * place[0] + 4 * h + 2 * u + p, 0))
    in_specs = [
        pl.BlockSpec((256, 256), lambda p, place: (0, 0)),
        pl.BlockSpec((16, 16, WIDE), lambda p, place: (2 * u + p, 0, 0)),
        own,
        pl.BlockSpec((8, 32, HALF), lambda p, place: (0, 2 * u + p, 0)),
        gate, gate, weight, weight, weight, weight,
    ]
    operands = [perm, received, tokens, far_tokens, *gates, *ups, *downs]
    aliases = {}
    if whole is not None:
        aliases = {len(operands) + 1: 0}
        in_specs.append(pl.BlockSpec(memory_space=pl.ANY))
        operands.append(whole)
    return pl.pallas_call(
        mixer_kernel,
        grid_spec=pltpu.PrefetchScalarGridSpec(
            num_scalar_prefetch=1,
            grid=(2,),
            in_specs=in_specs,
            out_specs=[own, pl.BlockSpec((8, 32, HALF), lambda p, place: (0, p, 0))],
            scratch_shapes=[pltpu.VMEM((2, 256, HALF), jnp.bfloat16)],
        ),
        out_shape=[
            jax.ShapeDtypeStruct((8, 512, HALF), jnp.bfloat16),
            jax.ShapeDtypeStruct((8, 64, HALF), jnp.bfloat16),
        ],
        input_output_aliases=aliases,
        compiler_params=pltpu.CompilerParams(vmem_limit_bytes=VMEM),
        cost_estimate=pl.CostEstimate(
            flops=6_000_000_000, bytes_accessed=14_000_000, transcendentals=4_000_000
        ),
        name="channel_mix",
    )(place, *operands)


def swap(value):
    return lax.ppermute(value, "ch", [(0, 1), (1, 0)])


def swap_cores(value):
    return lax.ppermute(value, "ctx", [(i, i ^ 1) for i in range(N_CTX)])


def exponent_route(step):
    pairs = []
    for i0 in range(N_CTX):
        for c0 in range(2):
            s, h = i0 // 32, (i0 // 16) % 2
            i = 4 * (i0 % 16) + ((2 * h + c0) ^ step)
            pairs.append((2 * i0 + c0, 2 * i + (s ^ z_hi(i))))
    return pairs


def routed_exponents(second_exponents, ctx, ch):
    columns = second_exponents.transpose(2, 1, 0)
    source = 2 * ((ctx // 16) % 2) + ch
    got = []
    for step in range(4):
        rows = lax.dynamic_slice_in_dim(columns, 2 * (source ^ step), 2, 1)
        got.append(lax.ppermute(rows, BOTH, exponent_route(step)))

    def finish():
        stacked = jnp.stack(got)
        ordered = jnp.stack(
            [lax.dynamic_index_in_dim(stacked, v ^ (ctx % 4), 0, keepdims=False) for v in range(4)]
        )
        split = ordered.reshape(2, 2, 6, 2, N_CTX, 8)
        return split.transpose(0, 1, 2, 4, 3, 5).reshape(2, 6, 2, 1024)

    return got, finish


def doubled_mix(mix):
    row = lax.broadcasted_iota(jnp.int32, (1024, 512), 0)
    col = lax.broadcasted_iota(jnp.int32, (1024, 512), 1)
    pick = ((row // 16) * 8 + row % 8 == col).astype(jnp.bfloat16)
    tall = jnp.dot(pick, mix, preferred_element_type=jnp.float32).astype(jnp.bfloat16)
    full = lax.dot_general(tall, pick, (((1,), (1,)), ((), ())), preferred_element_type=jnp.float32)
    row = lax.broadcasted_iota(jnp.int32, (1024, 1024), 0)
    col = lax.broadcasted_iota(jnp.int32, (1024, 1024), 1)
    return jnp.where((row // 8) % 2 == (col // 8) % 2, full, 0.0).astype(jnp.bfloat16)


def body(
    tokens,
    mix_first,
    mix_second,
    spectral_kernel,
    gate_scale,
    up_weight,
    down_weight,
    first_exponents,
    second_exponents,
):
    ctx = lax.axis_index("ctx")
    ch = lax.axis_index("ch")
    core = ctx % 2
    side = ch ^ ((ctx // 8) % 2)
    place = jnp.stack([side, ch]).astype(jnp.int32)
    perm = regroup_matrix()

    rows = 2 * BW
    piece = rows // 16
    start = ((ctx // 16) * 4 + (ctx % 8) // 2) * piece
    cut = lambda w: lax.dynamic_slice_in_dim(w.reshape(rows, 4, BW), start, piece, 0).reshape(piece, WIDE)
    slice_far = swap(jnp.where(core == 0, cut(up_weight), cut(down_weight)))
    own_gate = gate_scale.reshape(1, HALF)
    far_gate = swap(own_gate)
    exps, finish_exps = routed_exponents(second_exponents, ctx, ch)

    send = first_stage(
        mix_first,
        jnp.asarray(perm, jnp.bfloat16),
        tokens,
        spectral_kernel,
        first_exponents.transpose(2, 0, 1),
    )
    send, slice_far, far_gate, exps[:] = lax.optimization_barrier((send, slice_far, far_gate, list(exps)))
    gathered = lax.all_gather(slice_far, "ctx", axis=0, tiled=True, axis_index_groups=PLANES)
    received = lax.all_to_all(
        send.reshape(128, 2, 16, HALF), BOTH, split_axis=0, concat_axis=0, tiled=True
    ).reshape(N_CTX, 2, 2, 16, HALF)

    crossed = swap_cores(gathered)
    whole_shape = (2, BW, WIDE)
    far_up = jnp.where(core == 0, gathered, crossed).reshape(whole_shape)
    far_down = jnp.where(core == 0, crossed, gathered).reshape(whole_shape)
    ups = (up_weight.reshape(whole_shape), far_up)
    downs = (down_weight.reshape(whole_shape), far_down)
    gates = (own_gate, far_gate)
    mix = doubled_mix(mix_second)
    tops = finish_exps()

    far_tokens = [swap(part) for part in peel_stage(place, tokens, received)]
    whole = None
    back = []
    perm_back = jnp.asarray(perm.T, jnp.bfloat16)
    for h in range(2):
        second = second_stage(mix, received, tops, h)
        mixed = lax.all_to_all(
            second, BOTH, split_axis=0, concat_axis=0, tiled=True, axis_index_groups=SIDES
        )
        for u in range(2):
            whole, far = mixer_stage(
                place, perm_back, mixed, tokens, far_tokens[h], gates, ups, downs, whole, h, u
            )
            back.append(swap(far))
    for n, part in enumerate(back):
        whole = lax.dynamic_update_slice_in_dim(whole, part, (1 - side) * 256 + 64 * n, 1)
    return whole


def solution(mesh):
    placed = (
        P("ctx", None, "ch"),
        P(),
        P(),
        P("ctx", None, "ch"),
        P("ch"),
        P("ch", None, None, None),
        P("ch", None, None, None),
        P("ctx", None, "ch"),
        P(None, "ctx", "ch"),
    )
    return jax.shard_map(
        body, mesh=mesh, in_specs=placed, out_specs=P("ctx", None, "ch"), check_vma=False
    )
```

```python
import jax
import jax.numpy as jnp
import numpy as np
from jax import lax
from jax.experimental import pallas as pl
from jax.experimental.pallas import tpu as pltpu
from jax.sharding import PartitionSpec as P


BLK = 128
HALF = 768
BW = 384
WIDE = 1536
VMEM = 56 * 1024 * 1024
BOTH = ("ctx", "ch")
N_CTX = 64


def z_hi(i):
    return (i // 8) % 2


SIDES = [[2 * i + (s ^ z_hi(i)) for i in range(N_CTX)] for s in range(2)]
PLANES = [[i for i in range(N_CTX) if z_hi(i) == z and i % 2 == core] for z in range(2) for core in range(2)]


def limits(exponent):
    return lax.shift_left(jnp.ones_like(exponent), exponent + 9).astype(jnp.float32) * 0.875


def regroup_matrix():
    matrix = np.zeros((256, 256), np.float32)
    for i in range(16):
        for r in range(2):
            for a in range(8):
                matrix[i * 16 + r * 8 + a, a * 32 + i * 2 + r] = 1.0
    return matrix


def first_kernel(mix_ref, perm_ref, tok_ref, spec_ref, exp_ref, out_ref, enc_ref):
    columns = limits(exp_ref[0]).T
    mix = mix_ref[...]
    for pair in range(4):
        rhs = jnp.concatenate([tok_ref[2 * pair], tok_ref[2 * pair + 1]], axis=1)
        acc = jnp.dot(mix, rhs, preferred_element_type=jnp.float32)
        for side in range(2):
            a = 2 * pair + side
            value = acc[:, side * BLK:(side + 1) * BLK] * spec_ref[a].astype(jnp.float32)
            top = columns[:, a:a + 1]
            enc_ref[a] = jnp.clip(value, -top, top).astype(jnp.bfloat16)
    for g in range(4):
        for h in range(2):
            both = jnp.concatenate(
                [
                    enc_ref[:, s * 256 + h * 128 + g * 32:s * 256 + h * 128 + (g + 1) * 32, :].reshape(256, BLK)
                    for s in range(2)
                ],
                axis=1,
            )
            moved = jnp.dot(perm_ref[...], both, preferred_element_type=jnp.float32).astype(jnp.bfloat16)
            for s in range(2):
                cols = slice(s * BLK, (s + 1) * BLK)
                out_ref[g * 16:g * 16 + 8, s, h] = moved[:128, cols].reshape(8, 16, BLK)
                out_ref[g * 16 + 8:g * 16 + 16, 1 - s, h] = moved[128:, cols].reshape(8, 16, BLK)


def first_stage(mix_first, perm, tokens, spectral, exponents):
    wide = pl.BlockSpec((8, 512, BLK), lambda d: (0, 0, d))
    return pl.pallas_call(
        first_kernel,
        grid=(HALF // BLK,),
        in_specs=[
            pl.BlockSpec((512, 512), lambda d: (0, 0)),
            pl.BlockSpec((256, 256), lambda d: (0, 0)),
            wide,
            wide,
            pl.BlockSpec((1, 8, 512), lambda d: (d, 0, 0)),
        ],
        out_specs=pl.BlockSpec((N_CTX, 2, 2, 16, BLK), lambda d: (0, 0, 0, 0, d)),
        out_shape=jax.ShapeDtypeStruct((N_CTX, 2, 2, 16, HALF), jnp.bfloat16),
        scratch_shapes=[pltpu.VMEM((8, 512, BLK), jnp.bfloat16)],
        compiler_params=pltpu.CompilerParams(vmem_limit_bytes=VMEM),
        cost_estimate=pl.CostEstimate(flops=4_800_000_000, bytes_accessed=18_900_000, transcendentals=0),
        name="first_mix",
    )(mix_first, perm, tokens, spectral, exponents)


def second_kernel(mix_ref, recv_ref, exp_ref, out_ref):
    columns = limits(exp_ref[0, 0]).T
    mix = mix_ref[...]
    both = recv_ref[:, 0, 0].astype(jnp.float32)
    parts = []
    for r in range(2):
        right = both[:, r * 8:(r + 1) * 8, :].reshape(512, HALF).astype(jnp.bfloat16)
        parts.append(jnp.dot(mix, right, preferred_element_type=jnp.float32))
    for n in range(6):
        cols = slice(n * BLK, (n + 1) * BLK)
        held = []
        for r in range(2):
            top = columns[:, 2 * n + r:2 * n + r + 1]
            held.append(jnp.clip(parts[r][:, cols], -top, top).reshape(N_CTX, 8, BLK))
        out_ref[:, :, cols] = jnp.concatenate(held, axis=1).astype(jnp.bfloat16)


def second_stage(mix, received, exponents, h):
    return pl.pallas_call(
        second_kernel,
        grid=(2,),
        in_specs=[
            pl.BlockSpec((512, 512), lambda c: (0, 0)),
            pl.BlockSpec((N_CTX, 1, 1, 16, HALF), lambda c: (0, c, h, 0, 0)),
            pl.BlockSpec((1, 1, 12, 512), lambda c: (h, c, 0, 0)),
        ],
        out_specs=pl.BlockSpec((N_CTX, 16, HALF), lambda c: (0, 0, c)),
        out_shape=jax.ShapeDtypeStruct((N_CTX, 16, WIDE), jnp.bfloat16),
        compiler_params=pltpu.CompilerParams(vmem_limit_bytes=VMEM),
        cost_estimate=pl.CostEstimate(flops=1_600_000_000, bytes_accessed=7_000_000, transcendentals=0),
        name="second_mix",
    )(mix, received, exponents)


def mixer_kernel(
    place_ref, perm_ref, recv_ref, own_tok_ref, far_tok_ref, gate_ref, up_ref, down_ref, *rest
):
    own_out_ref, far_out_ref, gated_ref, total_ref = rest[-4:]
    c = place_ref[1]
    p = pl.program_id(0)
    q = pl.program_id(1)

    def gate_half(half, tok_ref):
        start = pl.multiple_of((c if half == 0 else 1 - c) * HALF, BLK)
        for g in range(2):
            mixed = jnp.dot(
                perm_ref[...],
                recv_ref[g * 16:(g + 1) * 16, :, pl.ds(start, HALF)].reshape(256, HALF),
                preferred_element_type=jnp.float32,
            )
            tok = tok_ref[:, g * 32:(g + 1) * 32, :].reshape(256, HALF).astype(jnp.float32)
            slope = jax.nn.sigmoid(tok * gate_ref[half:half + 1, :])
            gated_ref[half, g * 256:(g + 1) * 256, :] = (tok + mixed * slope).astype(jnp.bfloat16)

    @pl.when((p == 0) & (q == 0))
    def _():
        gate_half(0, own_tok_ref)

    @pl.when((p == 1) & (q == 0))
    def _():
        gate_half(1, far_tok_ref)

    hidden = []
    for i in range(2):
        pre = jnp.dot(
            gated_ref[p, :, i * BW:(i + 1) * BW], up_ref[0, i], preferred_element_type=jnp.float32
        )
        hidden.append(jax.nn.gelu(pre, approximate=True).astype(jnp.bfloat16))
    parts = []
    for k in range(2):
        cols = slice(k * BW, (k + 1) * BW)
        left = jnp.concatenate([part[:, cols] for part in hidden], axis=1)
        right = down_ref[0, :, :, cols].reshape(HALF, BW)
        parts.append(jnp.dot(left, right, preferred_element_type=jnp.float32))

    @pl.when(p == 0)
    def _():
        for k in range(2):
            total_ref[q, :, k * BW:(k + 1) * BW] = parts[k]

    def finish(half, out_ref):
        for k in range(2):
            cols = slice(k * BW, (k + 1) * BW)
            result = gated_ref[half, :, cols].astype(jnp.float32) + total_ref[half, :, cols] + parts[k]
            result = result.astype(jnp.bfloat16)
            for g in range(2):
                out_ref[:, g * 32:(g + 1) * 32, cols] = result[g * 256:(g + 1) * 256].reshape(8, 32, BW)

    @pl.when((p == 1) & (q == 0))
    def _():
        finish(0, own_out_ref)

    @pl.when((p == 1) & (q == 1))
    def _():
        finish(1, far_out_ref)


def mixer_stage(place, perm, received, tokens, far_tokens, gates, ups, downs, whole, n):
    weight = pl.BlockSpec((1, 2, BW, HALF), lambda p, q, place: (p, 0, 0, (place[1] + q) % 2))
    own = pl.BlockSpec((8, 64, HALF), lambda p, q, place: (0, 4 * place[0] + n, 0))
    far = pl.BlockSpec((8, 64, HALF), lambda p, q, place: (0, 0, 0))
    far_in = pl.BlockSpec((8, 64, HALF), lambda p, q, place: (0, 0, 0))
    in_specs = [
        pl.BlockSpec((256, 256), lambda p, q, place: (0, 0)),
        pl.BlockSpec((32, 16, WIDE), lambda p, q, place: (n % 2, 0, 0)),
        own,
        far_in,
        pl.BlockSpec((2, HALF), lambda p, q, place: (0, 0)),
        weight,
        weight,
    ]
    operands = [perm, received, tokens, far_tokens, gates, ups, downs]
    aliases = {}
    if whole is not None:
        aliases = {len(operands) + 1: 0}
        in_specs.append(pl.BlockSpec(memory_space=pl.ANY))
        operands.append(whole)
    return pl.pallas_call(
        mixer_kernel,
        grid_spec=pltpu.PrefetchScalarGridSpec(
            num_scalar_prefetch=1,
            grid=(2, 2),
            in_specs=in_specs,
            out_specs=[own, far],
            scratch_shapes=[
                pltpu.VMEM((2, 512, HALF), jnp.bfloat16),
                pltpu.VMEM((2, 512, HALF), jnp.float32),
            ],
        ),
        out_shape=[
            jax.ShapeDtypeStruct((8, 512, HALF), jnp.bfloat16),
            jax.ShapeDtypeStruct((8, 64, HALF), jnp.bfloat16),
        ],
        input_output_aliases=aliases,
        compiler_params=pltpu.CompilerParams(vmem_limit_bytes=VMEM),
        cost_estimate=pl.CostEstimate(
            flops=5_200_000_000, bytes_accessed=16_000_000, transcendentals=4_000_000
        ),
        name="channel_mix",
    )(place, *operands)


def swap(value):
    return lax.ppermute(value, "ch", [(0, 1), (1, 0)])


def swap_cores(value):
    return lax.ppermute(value, "ctx", [(i, i ^ 1) for i in range(N_CTX)])


def exponent_route(step):
    pairs = []
    for i0 in range(N_CTX):
        for c0 in range(2):
            s, h = i0 // 32, (i0 // 16) % 2
            i = 4 * (i0 % 16) + ((2 * h + c0) ^ step)
            pairs.append((2 * i0 + c0, 2 * i + (s ^ z_hi(i))))
    return pairs


def routed_exponents(second_exponents, ctx, ch):
    columns = second_exponents.transpose(2, 1, 0)
    source = 2 * ((ctx // 16) % 2) + ch
    got = []
    for step in range(4):
        rows = lax.dynamic_slice_in_dim(columns, 2 * (source ^ step), 2, 1)
        got.append(lax.ppermute(rows, BOTH, exponent_route(step)))

    def finish():
        stacked = jnp.stack(got)
        ordered = jnp.stack(
            [lax.dynamic_index_in_dim(stacked, v ^ (ctx % 4), 0, keepdims=False) for v in range(4)]
        )
        return ordered.reshape(2, 2, 12, 512)

    return got, finish


def body(
    tokens,
    mix_first,
    mix_second,
    spectral_kernel,
    gate_scale,
    up_weight,
    down_weight,
    first_exponents,
    second_exponents,
):
    ctx = lax.axis_index("ctx")
    ch = lax.axis_index("ch")
    core = ctx % 2
    side = ch ^ ((ctx // 8) % 2)
    place = jnp.stack([side, ch]).astype(jnp.int32)
    perm = regroup_matrix()

    rows = 2 * BW
    piece = rows // 16
    start = ((ctx // 16) * 4 + (ctx % 8) // 2) * piece
    cut = lambda w: lax.dynamic_slice_in_dim(w.reshape(rows, 4, BW), start, piece, 0).reshape(piece, WIDE)
    slice_far = swap(jnp.where(core == 0, cut(up_weight), cut(down_weight)))
    own_gate = gate_scale.reshape(1, HALF)
    far_gate = swap(own_gate)
    exps, finish_exps = routed_exponents(second_exponents, ctx, ch)

    send = first_stage(
        mix_first,
        jnp.asarray(perm, jnp.bfloat16),
        tokens,
        spectral_kernel,
        first_exponents.transpose(2, 0, 1),
    )
    send, slice_far, far_gate = lax.optimization_barrier((send, slice_far, far_gate))
    gathered = lax.all_gather(slice_far, "ctx", axis=0, tiled=True, axis_index_groups=PLANES)
    received = lax.all_to_all(
        send.reshape(128, 2, 16, HALF), BOTH, split_axis=0, concat_axis=0, tiled=True
    ).reshape(N_CTX, 2, 2, 16, HALF)

    whole_shape = (2, BW, WIDE)
    gates = jnp.concatenate([own_gate, far_gate], axis=0)
    tops = finish_exps()
    own_up = up_weight.reshape(whole_shape)
    own_down = down_weight.reshape(whole_shape)

    peel = lambda n: lax.dynamic_slice_in_dim(tokens, (1 - side) * 256 + 64 * n, 64, 1)
    far_tokens = [swap(peel(0))]
    peeled = [peel(n) for n in range(1, 4)]
    received, far_tokens[0], peeled, own_up, own_down, tops, gates = lax.optimization_barrier(
        (received, far_tokens[0], peeled, own_up, own_down, tops, gates)
    )
    far_tokens += [swap(part) for part in peeled]

    second = [second_stage(mix_second, received, tops, h) for h in range(2)]
    mixed0 = lax.all_to_all(
        second[0], BOTH, split_axis=0, concat_axis=0, tiled=True, axis_index_groups=SIDES
    )
    gathered, _ = lax.optimization_barrier((gathered, second[0]))
    crossed = swap_cores(gathered)
    far_up = jnp.where(core == 0, gathered, crossed).reshape(whole_shape)
    far_down = jnp.where(core == 0, crossed, gathered).reshape(whole_shape)
    ups = jnp.stack([own_up, far_up])
    downs = jnp.stack([own_down, far_down])
    mixed0, ups, downs, second[1], far_tokens[1], far_tokens[2] = lax.optimization_barrier(
        (mixed0, ups, downs, second[1], far_tokens[1], far_tokens[2])
    )
    mixed1 = lax.all_to_all(
        second[1], BOTH, split_axis=0, concat_axis=0, tiled=True, axis_index_groups=SIDES
    )
    whole = None
    back = []
    perm_back = jnp.asarray(perm.T, jnp.bfloat16)

    def place_part(whole, n):
        return lax.dynamic_update_slice_in_dim(whole, back[n], (1 - side) * 256 + 64 * n, 1)

    for n in range(4):
        if n == 3:
            whole = place_part(whole, 0)
        whole, far = mixer_stage(
            place, perm_back, (mixed0, mixed1)[n // 2], tokens, far_tokens[n], gates, ups, downs, whole, n
        )
        back.append(swap(far))
    for n in range(1, 4):
        whole = place_part(whole, n)
    return whole


def solution(mesh):
    placed = (
        P("ctx", None, "ch"),
        P(),
        P(),
        P("ctx", None, "ch"),
        P("ch"),
        P("ch", None, None, None),
        P("ch", None, None, None),
        P("ctx", None, "ch"),
        P(None, "ctx", "ch"),
    )
    return jax.shard_map(
        body, mesh=mesh, in_specs=placed, out_specs=P("ctx", None, "ch"), check_vma=False
    )
```

```python
import jax
import jax.numpy as jnp
import numpy as np
from jax import lax
from jax.experimental import pallas as pl
from jax.experimental.pallas import tpu as pltpu
from jax.sharding import PartitionSpec as P


BLK = 128
HALF = 768
BW = 384
WIDE = 1536
VMEM = 56 * 1024 * 1024
BOTH = ("ctx", "ch")
N_CTX = 64


def z_hi(i):
    return (i // 8) % 2


SIDES = [[2 * i + (s ^ z_hi(i)) for i in range(N_CTX)] for s in range(2)]
PLANES = [[i for i in range(N_CTX) if z_hi(i) == z and i % 2 == core] for z in range(2) for core in range(2)]


def limits(exponent):
    return lax.shift_left(jnp.ones_like(exponent), exponent + 9).astype(jnp.float32) * 0.875


def regroup_matrix():
    matrix = np.zeros((256, 256), np.float32)
    for i in range(16):
        for r in range(2):
            for a in range(8):
                matrix[i * 16 + r * 8 + a, a * 32 + i * 2 + r] = 1.0
    return matrix


def first_kernel(mix_ref, perm_ref, tok_ref, spec_ref, exp_ref, out_ref, enc_ref):
    rhs = jnp.concatenate([tok_ref[a] for a in range(8)], axis=1)
    acc = jnp.dot(mix_ref[...], rhs, preferred_element_type=jnp.float32)
    for n in range(2):
        columns = limits(exp_ref[n]).T
        cols = slice(n * BLK, (n + 1) * BLK)
        for a in range(8):
            first = a * 2 * BLK + n * BLK
            value = acc[:, first:first + BLK] * spec_ref[a, :, cols].astype(jnp.float32)
            top = columns[:, a:a + 1]
            enc_ref[a, :, cols] = jnp.clip(value, -top, top).astype(jnp.bfloat16)
    for g in range(4):
        for h in range(2):
            for s in range(2):
                first = s * 256 + h * 128 + g * 32
                part = enc_ref[:, first:first + 32, :].reshape(256, 2 * BLK)
                moved = jnp.dot(perm_ref[...], part, preferred_element_type=jnp.float32).astype(jnp.bfloat16)
                out_ref[g * 16:g * 16 + 8, s, h] = moved[:128].reshape(8, 16, 2 * BLK)
                out_ref[g * 16 + 8:g * 16 + 16, 1 - s, h] = moved[128:].reshape(8, 16, 2 * BLK)


def first_stage(mix_first, perm, tokens, spectral, exponents):
    wide = pl.BlockSpec((8, 512, 2 * BLK), lambda d: (0, 0, d))
    return pl.pallas_call(
        first_kernel,
        grid=(3,),
        in_specs=[
            pl.BlockSpec((512, 512), lambda d: (0, 0)),
            pl.BlockSpec((256, 256), lambda d: (0, 0)),
            wide,
            wide,
            pl.BlockSpec((2, 8, 512), lambda d: (d, 0, 0)),
        ],
        out_specs=pl.BlockSpec((N_CTX, 2, 2, 16, 2 * BLK), lambda d: (0, 0, 0, 0, d)),
        out_shape=jax.ShapeDtypeStruct((N_CTX, 2, 2, 16, HALF), jnp.bfloat16),
        scratch_shapes=[pltpu.VMEM((8, 512, 2 * BLK), jnp.bfloat16)],
        compiler_params=pltpu.CompilerParams(vmem_limit_bytes=VMEM),
        cost_estimate=pl.CostEstimate(flops=4_800_000_000, bytes_accessed=18_900_000, transcendentals=0),
        name="first_mix",
    )(mix_first, perm, tokens, spectral, exponents)


def second_kernel(mix_ref, recv_ref, top_ref, out_ref):
    columns = top_ref[0, 0].T
    mix = mix_ref[...]
    both = recv_ref[:, 0, 0].astype(jnp.float32)
    parts = []
    for r in range(2):
        right = both[:, r * 8:(r + 1) * 8, :].reshape(512, HALF).astype(jnp.bfloat16)
        parts.append(jnp.dot(mix, right, preferred_element_type=jnp.float32))
    for n in range(6):
        cols = slice(n * BLK, (n + 1) * BLK)
        held = []
        for r in range(2):
            top = columns[:, 2 * n + r:2 * n + r + 1]
            held.append(jnp.clip(parts[r][:, cols], -top, top).reshape(N_CTX, 8, BLK))
        out_ref[:, :, cols] = jnp.concatenate(held, axis=1).astype(jnp.bfloat16)


def second_stage(mix, received, tops, h):
    return pl.pallas_call(
        second_kernel,
        grid=(2,),
        in_specs=[
            pl.BlockSpec((512, 512), lambda c: (0, 0)),
            pl.BlockSpec((N_CTX, 1, 1, 16, HALF), lambda c: (0, c, h, 0, 0)),
            pl.BlockSpec((1, 1, 12, 512), lambda c: (h, c, 0, 0)),
        ],
        out_specs=pl.BlockSpec((N_CTX, 16, HALF), lambda c: (0, 0, c)),
        out_shape=jax.ShapeDtypeStruct((N_CTX, 16, WIDE), jnp.bfloat16),
        compiler_params=pltpu.CompilerParams(vmem_limit_bytes=VMEM),
        cost_estimate=pl.CostEstimate(flops=1_600_000_000, bytes_accessed=7_000_000, transcendentals=0),
        name="second_mix",
    )(mix, received, tops)


def mixer_kernel(
    place_ref, perm_ref, recv_ref, own_tok_ref, far_tok_ref, gate_ref, own_up_ref, own_down_ref,
    same_ref, cross_ref, *rest
):
    own_out_ref, far_out_ref, gated_ref, total_ref, far_ref, sems = rest[-6:]
    c = place_ref[1]
    core = place_ref[2]
    p = pl.program_id(0)
    q = pl.program_id(1)

    copies = [
        pltpu.make_async_copy(ref, far_ref.at[n], sems.at[n]) for n, ref in enumerate((same_ref, cross_ref))
    ]

    def gate_half(half, tok_ref):
        for g in range(2):
            mixed = jnp.dot(
                perm_ref[...],
                recv_ref[g * 16:(g + 1) * 16].reshape(256, HALF),
                preferred_element_type=jnp.float32,
            )
            tok = tok_ref[:, g * 32:(g + 1) * 32, :].reshape(256, HALF).astype(jnp.float32)
            slope = jax.nn.sigmoid(tok * gate_ref[half:half + 1, :])
            gated_ref[half, g * 256:(g + 1) * 256, :] = (tok + mixed * slope).astype(jnp.bfloat16)

    def mix(inputs, ups, downs):
        hidden = []
        for left, up in zip(inputs, ups):
            pre = jnp.dot(left, up, preferred_element_type=jnp.float32)
            hidden.append(jax.nn.gelu(pre, approximate=True).astype(jnp.bfloat16))
        parts = []
        for k in range(2):
            cols = slice(k * BW, (k + 1) * BW)
            left = jnp.concatenate([part[:, cols] for part in hidden], axis=1)
            right = jnp.concatenate([down[:, cols] for down in downs], axis=0)
            parts.append(jnp.dot(left, right, preferred_element_type=jnp.float32))
        return parts

    @pl.when((p == 0) & (q == 0))
    def _():
        for copy in copies:
            copy.start()
        gate_half(0, own_tok_ref)

    @pl.when((p == 1) & (q == 0))
    def _():
        gate_half(1, far_tok_ref)
        for copy in copies:
            copy.wait()

    @pl.when(p == 0)
    def _():
        parts = mix(
            [gated_ref[0, :, i * BW:(i + 1) * BW] for i in range(2)],
            [own_up_ref[i] for i in range(2)],
            [own_down_ref[i] for i in range(2)],
        )
        for k in range(2):
            total_ref[q, :, k * BW:(k + 1) * BW] = parts[k]

    def finish(half, out_ref):
        start = (c if half == 0 else 1 - c) * HALF
        up_cols = pl.ds(pl.multiple_of(start, BLK), HALF)
        down_cols = pl.ds(pl.multiple_of(WIDE + start, BLK), HALF)
        parts = mix(
            [gated_ref[1, :, pl.ds(pl.multiple_of(i * BW, BLK), BW)] for i in (core, 1 - core)],
            [far_ref[n, :, up_cols] for n in range(2)],
            [far_ref[n, :, down_cols] for n in range(2)],
        )
        for k in range(2):
            cols = slice(k * BW, (k + 1) * BW)
            result = gated_ref[half, :, cols].astype(jnp.float32) + total_ref[half, :, cols] + parts[k]
            result = result.astype(jnp.bfloat16)
            for g in range(2):
                out_ref[:, g * 32:(g + 1) * 32, cols] = result[g * 256:(g + 1) * 256].reshape(8, 32, BW)

    @pl.when((p == 1) & (q == 0))
    def _():
        finish(0, own_out_ref)

    @pl.when((p == 1) & (q == 1))
    def _():
        finish(1, far_out_ref)


def mixer_stage(place, perm, received, tokens, far_tokens, block, gates, own_weights, far_weights, whole, n):
    own_weight = pl.BlockSpec((2, BW, HALF), lambda p, q, place: (0, 0, (place[1] + q * (1 - p) + p) % 2))
    far_weight = pl.BlockSpec(memory_space=pl.ANY)
    own = pl.BlockSpec((8, 64, HALF), lambda p, q, place: (0, 4 * place[0] + n, 0))
    far = pl.BlockSpec((8, 64, HALF), lambda p, q, place: (0, 0, 0))
    far_in = pl.BlockSpec((8, 64, HALF), lambda p, q, place: (0, block, 0))
    in_specs = [
        pl.BlockSpec((256, 256), lambda p, q, place: (0, 0)),
        pl.BlockSpec((32, 16, HALF), lambda p, q, place: (n % 2, 0, (place[1] + p) % 2)),
        own,
        far_in,
        pl.BlockSpec((2, HALF), lambda p, q, place: (0, 0)),
        own_weight, own_weight, far_weight, far_weight,
    ]
    operands = [perm, received, tokens, far_tokens, gates, *own_weights, *far_weights]
    aliases = {}
    if whole is not None:
        aliases = {len(operands) + 1: 0}
        in_specs.append(pl.BlockSpec(memory_space=pl.ANY))
        operands.append(whole)
    return pl.pallas_call(
        mixer_kernel,
        grid_spec=pltpu.PrefetchScalarGridSpec(
            num_scalar_prefetch=1,
            grid=(2, 2),
            in_specs=in_specs,
            out_specs=[own, far],
            scratch_shapes=[
                pltpu.VMEM((2, 512, HALF), jnp.bfloat16),
                pltpu.VMEM((2, 512, HALF), jnp.float32),
                pltpu.VMEM((2, BW, 2 * WIDE), jnp.bfloat16),
                pltpu.SemaphoreType.DMA((2,)),
            ],
        ),
        out_shape=[
            jax.ShapeDtypeStruct((8, 512, HALF), jnp.bfloat16),
            jax.ShapeDtypeStruct((8, 64, HALF), jnp.bfloat16),
        ],
        input_output_aliases=aliases,
        compiler_params=pltpu.CompilerParams(vmem_limit_bytes=VMEM),
        cost_estimate=pl.CostEstimate(
            flops=5_200_000_000, bytes_accessed=16_000_000, transcendentals=4_000_000
        ),
        name="channel_mix",
    )(place, *operands)


def swap(value):
    return lax.ppermute(value, "ch", [(0, 1), (1, 0)])


def swap_cores(value):
    return lax.ppermute(value, "ctx", [(i, i ^ 1) for i in range(N_CTX)])


def exponent_route(step):
    pairs = []
    for i0 in range(N_CTX):
        for c0 in range(2):
            s, h = i0 // 32, (i0 // 16) % 2
            i = 4 * (i0 % 16) + ((2 * h + c0) ^ step)
            pairs.append((2 * i0 + c0, 2 * i + (s ^ z_hi(i))))
    return pairs


def routed_limits(second_exponents, own_gate, ctx, ch):
    columns = limits(second_exponents.transpose(2, 1, 0))
    source = 2 * ((ctx // 16) % 2) + ch
    got = []
    for step in range(4):
        rows = lax.dynamic_slice_in_dim(columns, 2 * (source ^ step), 2, 1).reshape(12, 512)
        rows = jnp.concatenate([rows, own_gate], axis=0)
        got.append(lax.ppermute(rows, BOTH, exponent_route(step)))
    stacked = jnp.stack(got)
    ordered = [lax.dynamic_index_in_dim(stacked, v ^ (ctx % 4), 0, keepdims=False) for v in range(4)]
    gates = jnp.stack([ordered[0][12:], ordered[1][12:]])
    far_gate = lax.dynamic_index_in_dim(gates, 1 - ch, 0, keepdims=False).reshape(-1)[:HALF]
    tops = jnp.stack([part[:12] for part in ordered]).reshape(2, 2, 12, 512)
    return tops, far_gate.reshape(1, HALF)


def body(
    tokens,
    mix_first,
    mix_second,
    spectral_kernel,
    gate_scale,
    up_weight,
    down_weight,
    first_exponents,
    second_exponents,
):
    ctx = lax.axis_index("ctx")
    ch = lax.axis_index("ch")
    core = ctx % 2
    side = ch ^ ((ctx // 8) % 2)
    place = jnp.stack([side, ch, core]).astype(jnp.int32)
    perm = regroup_matrix()

    piece = BW // 16
    start = core * BW + ((ctx // 16) * 4 + (ctx % 8) // 2) * piece
    cut = lambda w: lax.dynamic_slice_in_dim(w.reshape(2 * BW, 4, BW), start, piece, 0).reshape(piece, WIDE)
    slice_far = swap(jnp.concatenate([cut(up_weight), cut(down_weight)], axis=1))
    own_gate = gate_scale.reshape(1, HALF)
    padded_gate = jnp.concatenate([own_gate, jnp.zeros((1, 256), jnp.float32)], axis=1).reshape(2, 512)
    tops, far_gate = routed_limits(second_exponents, padded_gate, ctx, ch)

    send = first_stage(
        mix_first,
        jnp.asarray(perm, jnp.bfloat16),
        tokens,
        spectral_kernel,
        first_exponents.transpose(2, 0, 1),
    )
    peel = lambda lo, hi: lax.dynamic_slice_in_dim(tokens, (1 - side) * 256 + lo, hi - lo, 1)
    far0 = swap(peel(0, 32))
    send, slice_far, far0 = lax.optimization_barrier((send, slice_far, far0))
    gathered = lax.all_gather(slice_far, "ctx", axis=0, tiled=True, axis_index_groups=PLANES)
    received = lax.all_to_all(
        send.reshape(128, 2, 16, HALF), BOTH, split_axis=0, concat_axis=0, tiled=True
    ).reshape(N_CTX, 2, 2, 16, HALF)

    whole_shape = (2, BW, WIDE)
    gates = jnp.concatenate([own_gate, far_gate], axis=0)
    own_up = up_weight.reshape(whole_shape)
    own_down = down_weight.reshape(whole_shape)

    far1 = swap(peel(32, 64))
    peeled = [peel(64, 192), peel(192, 256)]
    received, far1, peeled, own_up, own_down, tops, gates = lax.optimization_barrier(
        (received, far1, peeled, own_up, own_down, tops, gates)
    )
    far2, far3 = [swap(part) for part in peeled]

    second = [second_stage(mix_second, received, tops, h) for h in range(2)]
    mixed0 = lax.all_to_all(
        second[0], BOTH, split_axis=0, concat_axis=0, tiled=True, axis_index_groups=SIDES
    )
    gathered, _ = lax.optimization_barrier((gathered, second[0]))
    crossed = swap_cores(gathered)
    far_first = jnp.concatenate([far0, far1], axis=1)
    mixed0, second[1], far2, far_first = lax.optimization_barrier((mixed0, second[1], far2, far_first))
    far_tokens = ((far_first, 0), (far2, 0), (far2, 1), (far3, 0))
    mixed1 = lax.all_to_all(
        second[1], BOTH, split_axis=0, concat_axis=0, tiled=True, axis_index_groups=SIDES
    )
    whole = None
    back = []
    perm_back = jnp.asarray(perm.T, jnp.bfloat16)

    def place_part(whole, n):
        return lax.dynamic_update_slice_in_dim(whole, back[n], (1 - side) * 256 + 64 * n, 1)

    for n in range(4):
        if n == 3:
            whole = place_part(whole, 0)
        whole, far = mixer_stage(
            place, perm_back, (mixed0, mixed1)[n // 2], tokens, *far_tokens[n], gates,
            (own_up, own_down), (gathered, crossed), whole, n
        )
        back.append(swap(far))
    for n in range(1, 4):
        whole = place_part(whole, n)
    return whole


def solution(mesh):
    placed = (
        P("ctx", None, "ch"),
        P(),
        P(),
        P("ctx", None, "ch"),
        P("ch"),
        P("ch", None, None, None),
        P("ch", None, None, None),
        P("ctx", None, "ch"),
        P(None, "ctx", "ch"),
    )
    return jax.shard_map(
        body, mesh=mesh, in_specs=placed, out_specs=P("ctx", None, "ch"), check_vma=False
    )
```

```python
import jax
import jax.numpy as jnp
import numpy as np
from jax import lax
from jax.experimental import pallas as pl
from jax.experimental.pallas import tpu as pltpu
from jax.sharding import PartitionSpec as P


BLK = 128
HALF = 768
BW = 384
WIDE = 1536
VMEM = 56 * 1024 * 1024
BOTH = ("ctx", "ch")
N_CTX = 64


def z_hi(i):
    return (i // 8) % 2


SIDES = [[2 * i + (s ^ z_hi(i)) for i in range(N_CTX)] for s in range(2)]
PLANES = [[i for i in range(N_CTX) if z_hi(i) == z and i % 2 == core] for z in range(2) for core in range(2)]


def limits(exponent):
    return lax.shift_left(jnp.ones_like(exponent), exponent + 9).astype(jnp.float32) * 0.875


def regroup_matrix():
    matrix = np.zeros((256, 256), np.float32)
    for i in range(16):
        for r in range(2):
            for a in range(8):
                matrix[i * 16 + r * 8 + a, a * 32 + i * 2 + r] = 1.0
    return matrix


def first_kernel(mix_ref, perm_ref, tok_ref, spec_ref, exp_ref, out_ref, enc_ref):
    rhs = jnp.concatenate([tok_ref[a] for a in range(8)], axis=1)
    acc = jnp.dot(mix_ref[...], rhs, preferred_element_type=jnp.float32)
    for n in range(2):
        columns = limits(exp_ref[n]).T
        cols = slice(n * BLK, (n + 1) * BLK)
        for a in range(8):
            first = a * 2 * BLK + n * BLK
            value = acc[:, first:first + BLK] * spec_ref[a, :, cols].astype(jnp.float32)
            top = columns[:, a:a + 1]
            enc_ref[a, :, cols] = jnp.clip(value, -top, top).astype(jnp.bfloat16)
    for g in range(4):
        for h in range(2):
            for s in range(2):
                first = s * 256 + h * 128 + g * 32
                part = enc_ref[:, first:first + 32, :].reshape(256, 2 * BLK)
                moved = jnp.dot(perm_ref[...], part, preferred_element_type=jnp.float32).astype(jnp.bfloat16)
                out_ref[g * 16:g * 16 + 8, s, h] = moved[:128].reshape(8, 16, 2 * BLK)
                out_ref[g * 16 + 8:g * 16 + 16, 1 - s, h] = moved[128:].reshape(8, 16, 2 * BLK)


def first_stage(mix_first, perm, tokens, spectral, exponents):
    wide = pl.BlockSpec((8, 512, 2 * BLK), lambda d: (0, 0, d))
    return pl.pallas_call(
        first_kernel,
        grid=(3,),
        in_specs=[
            pl.BlockSpec((512, 512), lambda d: (0, 0)),
            pl.BlockSpec((256, 256), lambda d: (0, 0)),
            wide,
            wide,
            pl.BlockSpec((2, 8, 512), lambda d: (d, 0, 0)),
        ],
        out_specs=pl.BlockSpec((N_CTX, 2, 2, 16, 2 * BLK), lambda d: (0, 0, 0, 0, d)),
        out_shape=jax.ShapeDtypeStruct((N_CTX, 2, 2, 16, HALF), jnp.bfloat16),
        scratch_shapes=[pltpu.VMEM((8, 512, 2 * BLK), jnp.bfloat16)],
        compiler_params=pltpu.CompilerParams(vmem_limit_bytes=VMEM),
        cost_estimate=pl.CostEstimate(flops=4_800_000_000, bytes_accessed=18_900_000, transcendentals=0),
        name="first_mix",
    )(mix_first, perm, tokens, spectral, exponents)


def second_kernel(mix_ref, recv_ref, top_ref, out_ref):
    columns = top_ref[0, 0].T
    mix = mix_ref[...]
    both = recv_ref[:, 0, 0].astype(jnp.float32)
    parts = []
    for r in range(2):
        right = both[:, r * 8:(r + 1) * 8, :].reshape(512, HALF).astype(jnp.bfloat16)
        parts.append(jnp.dot(mix, right, preferred_element_type=jnp.float32))
    for n in range(6):
        cols = slice(n * BLK, (n + 1) * BLK)
        held = []
        for r in range(2):
            top = columns[:, 2 * n + r:2 * n + r + 1]
            held.append(jnp.clip(parts[r][:, cols], -top, top).reshape(N_CTX, 8, BLK))
        out_ref[:, :, cols] = jnp.concatenate(held, axis=1).astype(jnp.bfloat16)


def second_stage(mix, received, tops, h):
    return pl.pallas_call(
        second_kernel,
        grid=(2,),
        in_specs=[
            pl.BlockSpec((512, 512), lambda c: (0, 0)),
            pl.BlockSpec((N_CTX, 1, 1, 16, HALF), lambda c: (0, c, h, 0, 0)),
            pl.BlockSpec((1, 1, 12, 512), lambda c: (h, c, 0, 0)),
        ],
        out_specs=pl.BlockSpec((N_CTX, 16, HALF), lambda c: (0, 0, c)),
        out_shape=jax.ShapeDtypeStruct((N_CTX, 16, WIDE), jnp.bfloat16),
        compiler_params=pltpu.CompilerParams(vmem_limit_bytes=VMEM),
        cost_estimate=pl.CostEstimate(flops=1_600_000_000, bytes_accessed=7_000_000, transcendentals=0),
        name="second_mix",
    )(mix, received, tops)


def mixer_kernel(
    place_ref, perm_ref, recv_ref, own_tok_ref, far_tok_ref, gate_ref, own_up_ref, own_down_ref,
    same_ref, cross_ref, *rest
):
    own_out_ref, far_out_ref, gated_ref, total_ref, weight_ref, sems = rest[-6:]
    c = place_ref[1]
    core = place_ref[2]
    p = pl.program_id(0)
    q = pl.program_id(1)
    targets = (
        weight_ref.at[0, :, :, pl.ds(0, WIDE)],
        weight_ref.at[0, :, :, pl.ds(WIDE, WIDE)],
        weight_ref.at[1, 0],
        weight_ref.at[1, 1],
    )
    copies = [
        pltpu.make_async_copy(source, target, sems.at[n])
        for n, (source, target) in enumerate(zip((own_up_ref, own_down_ref, same_ref, cross_ref), targets))
    ]

    def gate_half(half, tok_ref):
        for g in range(2):
            mixed = jnp.dot(
                perm_ref[...], recv_ref[g * 16:(g + 1) * 16].reshape(256, HALF), preferred_element_type=jnp.float32
            )
            tok = tok_ref[:, g * 32:(g + 1) * 32, :].reshape(256, HALF).astype(jnp.float32)
            slope = jax.nn.sigmoid(tok * gate_ref[half:half + 1, :])
            gated_ref[half, g * 256:(g + 1) * 256, :] = (tok + mixed * slope).astype(jnp.bfloat16)

    @pl.when((p == 0) & (q == 0))
    def _():
        for copy in copies:
            copy.start()
        gate_half(0, own_tok_ref)
        for copy in copies[:2]:
            copy.wait()

    @pl.when((p == 1) & (q == 0))
    def _():
        gate_half(1, far_tok_ref)
        for copy in copies[2:]:
            copy.wait()

    half = (c + q) % 2
    up_cols = pl.ds(pl.multiple_of(half * HALF, BLK), HALF)
    hidden = []
    for i in range(2):
        first = jnp.where(p == 0, i, i ^ core) * BW
        pre = jnp.dot(
            gated_ref[p, :, pl.ds(pl.multiple_of(first, BLK), BW)],
            weight_ref[p, i, :, up_cols],
            preferred_element_type=jnp.float32,
        )
        hidden.append(jax.nn.gelu(pre, approximate=True).astype(jnp.bfloat16))
    for k in range(2):
        cols = slice(k * BW, (k + 1) * BW)
        left = jnp.concatenate([part[:, cols] for part in hidden], axis=1)
        down_cols = pl.ds(pl.multiple_of(WIDE + half * HALF + k * BW, BLK), BW)
        right = weight_ref[p, :, :, down_cols].reshape(HALF, BW)
        part = jnp.dot(left, right, preferred_element_type=jnp.float32)
        before = jnp.where(p == 0, 0.0, total_ref[q, :, cols] + gated_ref[q, :, cols].astype(jnp.float32))
        total_ref[q, :, cols] = part + before

    def finish(half, out_ref):
        for g in range(2):
            rows = total_ref[half, g * 256:(g + 1) * 256, :]
            out_ref[:, g * 32:(g + 1) * 32, :] = rows.astype(jnp.bfloat16).reshape(8, 32, HALF)

    @pl.when((p == 1) & (q == 0))
    def _():
        finish(0, own_out_ref)

    @pl.when((p == 1) & (q == 1))
    def _():
        finish(1, far_out_ref)


def mixer_stage(place, perm, received, tokens, far_tokens, block, gates, own_weights, far_weights, whole, n):
    weight = pl.BlockSpec(memory_space=pl.ANY)
    own = pl.BlockSpec((8, 64, HALF), lambda p, q, place: (0, 4 * place[0] + n, 0))
    far = pl.BlockSpec((8, 64, HALF), lambda p, q, place: (0, 0, 0))
    far_in = pl.BlockSpec((8, 64, HALF), lambda p, q, place: (0, block, 0))
    in_specs = [
        pl.BlockSpec((256, 256), lambda p, q, place: (0, 0)),
        pl.BlockSpec((32, 16, HALF), lambda p, q, place: (n % 2, 0, (place[1] + p) % 2)),
        own,
        far_in,
        pl.BlockSpec((2, HALF), lambda p, q, place: (0, 0)),
        weight, weight, weight, weight,
    ]
    operands = [perm, received, tokens, far_tokens, gates, *own_weights, *far_weights]
    aliases = {}
    if whole is not None:
        aliases = {len(operands) + 1: 0}
        in_specs.append(pl.BlockSpec(memory_space=pl.ANY))
        operands.append(whole)
    return pl.pallas_call(
        mixer_kernel,
        grid_spec=pltpu.PrefetchScalarGridSpec(
            num_scalar_prefetch=1,
            grid=(2, 2),
            in_specs=in_specs,
            out_specs=[own, far],
            scratch_shapes=[
                pltpu.VMEM((2, 512, HALF), jnp.bfloat16),
                pltpu.VMEM((2, 512, HALF), jnp.float32),
                pltpu.VMEM((2, 2, BW, 2 * WIDE), jnp.bfloat16),
                pltpu.SemaphoreType.DMA((4,)),
            ],
        ),
        out_shape=[
            jax.ShapeDtypeStruct((8, 512, HALF), jnp.bfloat16),
            jax.ShapeDtypeStruct((8, 64, HALF), jnp.bfloat16),
        ],
        input_output_aliases=aliases,
        compiler_params=pltpu.CompilerParams(vmem_limit_bytes=VMEM),
        cost_estimate=pl.CostEstimate(
            flops=5_200_000_000, bytes_accessed=16_000_000, transcendentals=4_000_000
        ),
        name="channel_mix",
    )(place, *operands)


def swap(value):
    return lax.ppermute(value, "ch", [(0, 1), (1, 0)])


def swap_cores(value):
    return lax.ppermute(value, "ctx", [(i, i ^ 1) for i in range(N_CTX)])


def exponent_route(step):
    pairs = []
    for i0 in range(N_CTX):
        for c0 in range(2):
            s, h = i0 // 32, (i0 // 16) % 2
            i = 4 * (i0 % 16) + ((2 * h + c0) ^ step)
            pairs.append((2 * i0 + c0, 2 * i + (s ^ z_hi(i))))
    return pairs


def routed_limits(second_exponents, own_gate, ctx, ch):
    columns = limits(second_exponents.transpose(2, 1, 0))
    source = 2 * ((ctx // 16) % 2) + ch
    got = []
    for step in range(4):
        rows = lax.dynamic_slice_in_dim(columns, 2 * (source ^ step), 2, 1).reshape(12, 512)
        rows = jnp.concatenate([rows, own_gate], axis=0)
        got.append(lax.ppermute(rows, BOTH, exponent_route(step)))
    stacked = jnp.stack(got)
    ordered = [lax.dynamic_index_in_dim(stacked, v ^ (ctx % 4), 0, keepdims=False) for v in range(4)]
    gates = jnp.stack([ordered[0][12:], ordered[1][12:]])
    far_gate = lax.dynamic_index_in_dim(gates, 1 - ch, 0, keepdims=False).reshape(-1)[:HALF]
    tops = jnp.stack([part[:12] for part in ordered]).reshape(2, 2, 12, 512)
    return tops, far_gate.reshape(1, HALF)


def body(
    tokens,
    mix_first,
    mix_second,
    spectral_kernel,
    gate_scale,
    up_weight,
    down_weight,
    first_exponents,
    second_exponents,
):
    ctx = lax.axis_index("ctx")
    ch = lax.axis_index("ch")
    core = ctx % 2
    side = ch ^ ((ctx // 8) % 2)
    place = jnp.stack([side, ch, core]).astype(jnp.int32)
    perm = regroup_matrix()

    piece = BW // 16
    start = core * BW + ((ctx // 16) * 4 + (ctx % 8) // 2) * piece
    cut = lambda w: lax.dynamic_slice_in_dim(w.reshape(2 * BW, 4, BW), start, piece, 0).reshape(piece, WIDE)
    slice_far = swap(jnp.concatenate([cut(up_weight), cut(down_weight)], axis=1))
    own_gate = gate_scale.reshape(1, HALF)
    padded_gate = jnp.concatenate([own_gate, jnp.zeros((1, 256), jnp.float32)], axis=1).reshape(2, 512)
    tops, far_gate = routed_limits(second_exponents, padded_gate, ctx, ch)

    send = first_stage(
        mix_first,
        jnp.asarray(perm, jnp.bfloat16),
        tokens,
        spectral_kernel,
        first_exponents.transpose(2, 0, 1),
    )
    peel = lambda lo, hi: lax.dynamic_slice_in_dim(tokens, (1 - side) * 256 + lo, hi - lo, 1)
    far0 = swap(peel(0, 32))
    send, slice_far, far0 = lax.optimization_barrier((send, slice_far, far0))
    gathered = lax.all_gather(slice_far, "ctx", axis=0, tiled=True, axis_index_groups=PLANES)
    received = lax.all_to_all(
        send.reshape(128, 2, 16, HALF), BOTH, split_axis=0, concat_axis=0, tiled=True
    ).reshape(N_CTX, 2, 2, 16, HALF)

    whole_shape = (2, BW, WIDE)
    gates = jnp.concatenate([own_gate, far_gate], axis=0)
    own_up = up_weight.reshape(whole_shape)
    own_down = down_weight.reshape(whole_shape)

    far1 = swap(peel(32, 64))
    peeled = [peel(64, 192), peel(192, 256)]
    received, far1, peeled, own_up, own_down, tops, gates = lax.optimization_barrier(
        (received, far1, peeled, own_up, own_down, tops, gates)
    )
    far2, far3 = [swap(part) for part in peeled]

    second = [second_stage(mix_second, received, tops, h) for h in range(2)]
    mixed0 = lax.all_to_all(
        second[0], BOTH, split_axis=0, concat_axis=0, tiled=True, axis_index_groups=SIDES
    )
    gathered, _ = lax.optimization_barrier((gathered, second[0]))
    crossed = swap_cores(gathered)
    far_first = jnp.concatenate([far0, far1], axis=1)
    mixed0, second[1], far2, far_first = lax.optimization_barrier((mixed0, second[1], far2, far_first))
    far_tokens = ((far_first, 0), (far2, 0), (far2, 1), (far3, 0))
    mixed1 = lax.all_to_all(
        second[1], BOTH, split_axis=0, concat_axis=0, tiled=True, axis_index_groups=SIDES
    )
    whole = None
    back = []
    perm_back = jnp.asarray(perm.T, jnp.bfloat16)

    def place_part(whole, n):
        return lax.dynamic_update_slice_in_dim(whole, back[n], (1 - side) * 256 + 64 * n, 1)

    for n in range(4):
        if n == 3:
            whole = place_part(whole, 0)
        whole, far = mixer_stage(
            place, perm_back, (mixed0, mixed1)[n // 2], tokens, *far_tokens[n], gates,
            (own_up, own_down), (gathered, crossed), whole, n
        )
        back.append(swap(far))
    for n in range(1, 4):
        whole = place_part(whole, n)
    return whole


def solution(mesh):
    placed = (
        P("ctx", None, "ch"),
        P(),
        P(),
        P("ctx", None, "ch"),
        P("ch"),
        P("ch", None, None, None),
        P("ch", None, None, None),
        P("ctx", None, "ch"),
        P(None, "ctx", "ch"),
    )
    return jax.shard_map(
        body, mesh=mesh, in_specs=placed, out_specs=P("ctx", None, "ch"), check_vma=False
    )
```
